128 devices in a mesh: wide: 8 (over z, core), narrow: 16 (over x, y).
Axes of the slice: x: 4, y: 4, z: 4, core: 2. Of those that a mesh axis runs over, the one named last changes fastest.
Arguments:
- tokens: bfloat16 [16384, 2048], P(('wide', 'narrow')), may hold values from -6 to 6
- out_grad: bfloat16 [16384, 2048], P(('wide', 'narrow')), may hold values from -6 to 6
- expert_ids: int32 [16384, 6], P(('wide', 'narrow')), may hold values from 0 to 63, as said below
- gates: bfloat16 [16384, 6], P(('wide', 'narrow')), may hold values from 0.049804688 to 0.5
- w_gate: bfloat16 [128, 2048, 704], P(('wide', 'narrow')), may hold values from -0.125 to 0.125
- w_up: bfloat16 [128, 2048, 704], P(('wide', 'narrow')), may hold values from -0.125 to 0.125
- w_down: bfloat16 [128, 704, 2048], P(('wide', 'narrow')), may hold values from -0.15625 to 0.15625
- gate_saved: bfloat16 [128, 1536, 704], P(('wide', 'narrow')), may hold values from -6 to 6
- up_saved: bfloat16 [128, 1536, 704], P(('wide', 'narrow')), may hold values from -6 to 6
Outputs:
- token_grad: bfloat16 [16384, 2048], P(('wide', 'narrow'))
- grad_gate: bfloat16 [128, 2048, 704], P(('wide', 'narrow'))
- grad_up: bfloat16 [128, 2048, 704], P(('wide', 'narrow'))
- grad_down: bfloat16 [128, 704, 2048], P(('wide', 'narrow'))
The draws below stay inside these ranges and needn't reach their ends.
Inputs may be any that keep to these rules, and one draw needn't show every extreme that they name: `expert_ids`: each row names 6 different experts, 2 in each of exactly 3 of the groups of 8 consecutive experts; for every device and every group, exactly 48 of the device's tokens name experts of that group.
All inputs are finite; a program needn't handle non-finite values.
Results may differ from the reference program's by a relative error of at most 0.012.
Values may be sent and summed in bfloat16 or wider, within the bound.
No kernel may reach another device: no remote copies, remote signals or barrier semaphores. Data moves between devices by JAX's collectives and lax.ppermute only.
A program may use at most 192 MiB of HBM per device.

```python
import math
import jax
import jax.numpy as jnp
from jax import lax

D = 2048
FF = 1408
TOP = 6
TOK_DEV = 128
NODES_MAX = 3
EXPERTS = 64
EXPERTS_NODE = 8
PER_NODE = 2
CAP = 12
HALF = 704
SLICES = 128
TOKENS = 16384
N_WIDE = 8
N_NARROW = 16


def draw_expert_ids(key, part):
    key = jax.random.fold_in(key, 11)
    key_offset, key_spots, key_level, key_noise = jax.random.split(key, 4)
    groups = EXPERTS // EXPERTS_NODE
    holders = TOKENS // TOK_DEV
    offset_score = jax.random.randint(key_offset, (holders, groups), 0, 4096) * groups + jnp.arange(groups, dtype=jnp.int32)[None, :]
    unused, offsets = lax.top_k(offset_score, NODES_MAX)
    spot_keys = jax.random.split(key_spots, holders)
    spots = jax.vmap(lambda k: jax.random.permutation(k, TOK_DEV))(spot_keys).astype(jnp.int32)
    base = spots % groups
    nodes = (base[:, :, None] + offsets[:, None, :].astype(jnp.int32)) % groups
    nodes = nodes.reshape(TOKENS, NODES_MAX)
    level = jax.random.randint(key_level, (EXPERTS,), 0, 4) * 1024
    noise = jax.random.randint(key_noise, (TOKENS, NODES_MAX, EXPERTS_NODE), 0, 2048)
    local_range = jnp.arange(EXPERTS_NODE, dtype=jnp.int32)
    expert_of = nodes[:, :, None] * EXPERTS_NODE + local_range[None, None, :]
    score = (level[expert_of] + noise) * EXPERTS_NODE + local_range[None, None, :]
    unused_two, local = lax.top_k(score, PER_NODE)
    picked = nodes[:, :, None] * EXPERTS_NODE + local.astype(jnp.int32)
    return picked.reshape(TOKENS, TOP).astype(jnp.int32)


def block_levels(rng, dims, cuts, least, largest):
    factor_of = 1.0
    for position, blocks in cuts:
        heights = jax.random.uniform(jax.random.fold_in(jax.random.fold_in(rng, 6), position), (blocks,), jnp.float32, least / len(cuts), largest / len(cuts))
        factor_of = factor_of * jnp.repeat(jnp.exp(heights), dims[position] // blocks).reshape((-1,) + (1,) * (len(dims) - 1 - position))
    return factor_of


def bell_draw(key, extent, deviation, most, cuts=(), kind=jnp.bfloat16):
    loudness = block_levels(key, extent, cuts, -0.22, 0.18) if cuts else 1.0
    drawn = jax.random.normal(key, extent, jnp.float32) * deviation * loudness
    return jnp.minimum(jnp.maximum(drawn, -most), most).astype(kind)


def setup_inputs(seed: int = 0) -> dict:
    key_list = jax.random.split(jax.random.key(seed), 10)
    tokens = bell_draw(key_list[0], (TOKENS, D), 1.0, 6.0, ((0, 128),))
    out_grad = bell_draw(key_list[1], (TOKENS, D), 1.0, 6.0, ((0, 128),))
    expert_ids = draw_expert_ids(jax.random.fold_in(key_list[9], 71), 0)
    gates = jnp.clip(jnp.exp(math.log(0.5) - 2.306499 * jax.random.uniform(key_list[3], (TOKENS, TOP), jnp.float32) ** block_levels(key_list[3], (TOKENS, TOP), ((0, 128),), -0.2, 0.2)), 0.049804688, 0.5).astype(jnp.bfloat16)
    w_gate = bell_draw(key_list[4], (SLICES, D, HALF), D ** -0.5, 0.125, ((0, 128),))
    w_up = bell_draw(key_list[5], (SLICES, D, HALF), D ** -0.5, 0.125, ((0, 128),))
    w_down = bell_draw(key_list[6], (SLICES, HALF, D), FF ** -0.5, 0.15625, ((0, 128),))
    gate_saved = bell_draw(key_list[7], (SLICES, N_WIDE * N_NARROW * CAP, HALF), 1.0, 6.0, ((0, 128),))
    up_saved = bell_draw(key_list[8], (SLICES, N_WIDE * N_NARROW * CAP, HALF), 1.0, 6.0, ((0, 128),))
    return dict(tokens=tokens, out_grad=out_grad, expert_ids=expert_ids, gates=gates, w_gate=w_gate, w_up=w_up, w_down=w_down, gate_saved=gate_saved, up_saved=up_saved)


def slot_tables(ids, gate_rows, experts, slot_cap):
    count = ids.shape[0]
    flat = ids.reshape(-1)
    picked = (flat[:, None] == jnp.arange(experts, dtype=jnp.int32)[None, :]).astype(jnp.int32)
    before = jnp.cumsum(picked, axis=0) - picked
    rank = jnp.sum(before * picked, axis=1)
    keep = rank < slot_cap
    place = flat * slot_cap + rank
    hits = (jnp.arange(experts * slot_cap, dtype=jnp.int32)[:, None] == place[None, :]) & keep[None, :]
    hits = hits.reshape(experts * slot_cap, count, ids.shape[1])
    placed = jnp.any(hits, axis=2).astype(jnp.float32)
    weighted = jnp.sum(jnp.where(hits, gate_rows[None, :, :], jnp.float32(0.0)), axis=2)
    return placed, weighted


def reference(tokens, out_grad, expert_ids, gates, w_gate, w_up, w_down, gate_saved, up_saved):
    devices = N_WIDE * N_NARROW
    experts = devices // 2
    high = lax.Precision.HIGHEST
    ids3 = expert_ids.reshape(devices, TOK_DEV, TOP)
    gates3 = gates.astype(jnp.float32).reshape(devices, TOK_DEV, TOP)
    placed, weighted = jax.vmap(lambda i, g: slot_tables(i, g, experts, CAP))(ids3, gates3)
    x32 = tokens.reshape(devices, TOK_DEV, D).astype(jnp.float32)
    dy32 = out_grad.reshape(devices, TOK_DEV, D).astype(jnp.float32)
    full_gate = w_gate.reshape(experts, 2, D, HALF).transpose(0, 2, 1, 3).reshape(experts, D, FF)
    full_up = w_up.reshape(experts, 2, D, HALF).transpose(0, 2, 1, 3).reshape(experts, D, FF)
    full_down = w_down.reshape(experts, FF, D)
    stored_gate = gate_saved.reshape(experts, 2, devices * CAP, HALF).transpose(0, 2, 1, 3).reshape(experts, devices * CAP, FF)
    stored_up = up_saved.reshape(experts, 2, devices * CAP, HALF).transpose(0, 2, 1, 3).reshape(experts, devices * CAP, FF)

    def one_expert(carry, expert):
        start = (expert * CAP).astype(jnp.int32)
        pick = lax.dynamic_slice_in_dim(placed, start, CAP, 1)
        scaled = lax.dynamic_slice_in_dim(weighted, start, CAP, 1)
        rows_x = jnp.einsum("sct,std->scd", pick, x32, precision=high).astype(jnp.bfloat16).reshape(-1, D)
        rows_dy = jnp.einsum("sct,std->scd", scaled, dy32, precision=high).astype(jnp.bfloat16).reshape(-1, D)
        wg = lax.dynamic_index_in_dim(full_gate, expert, 0, keepdims=False)
        wu = lax.dynamic_index_in_dim(full_up, expert, 0, keepdims=False)
        wd = lax.dynamic_index_in_dim(full_down, expert, 0, keepdims=False)
        gate_pre = lax.dynamic_index_in_dim(stored_gate, expert, 0, keepdims=False).astype(jnp.float32)
        up_pre = lax.dynamic_index_in_dim(stored_up, expert, 0, keepdims=False).astype(jnp.float32)
        sigma = jax.nn.sigmoid(gate_pre)
        silu = gate_pre * sigma
        act = (silu * up_pre).astype(jnp.bfloat16)
        act_grad = jnp.dot(rows_dy, wd.T, preferred_element_type=jnp.float32)
        up_grad = (act_grad * silu).astype(jnp.bfloat16)
        gate_grad = (act_grad * up_pre * sigma * (1.0 + gate_pre * (1.0 - sigma))).astype(jnp.bfloat16)
        slot_grad = jnp.dot(gate_grad, wg.T, preferred_element_type=jnp.float32) + jnp.dot(up_grad, wu.T, preferred_element_type=jnp.float32)
        back = jnp.einsum("sct,scd->std", pick, slot_grad.reshape(devices, CAP, D), precision=high)
        grad_one = jnp.dot(rows_x.T, gate_grad, preferred_element_type=jnp.float32).astype(jnp.bfloat16)
        grad_two = jnp.dot(rows_x.T, up_grad, preferred_element_type=jnp.float32).astype(jnp.bfloat16)
        grad_three = jnp.dot(act.T, rows_dy, preferred_element_type=jnp.float32).astype(jnp.bfloat16)
        return carry + back, (grad_one, grad_two, grad_three)

    start_carry = jnp.zeros((devices, TOK_DEV, D), jnp.float32)
    total, grads = lax.scan(one_expert, start_carry, jnp.arange(experts, dtype=jnp.int32))
    token_grad = total.reshape(devices * TOK_DEV, D).astype(jnp.bfloat16)
    grad_gate = grads[0].reshape(experts, D, 2, HALF).transpose(0, 2, 1, 3).reshape(devices, D, HALF)
    grad_up = grads[1].reshape(experts, D, 2, HALF).transpose(0, 2, 1, 3).reshape(devices, D, HALF)
    grad_down = grads[2].reshape(devices, HALF, D)
    return (token_grad, grad_gate, grad_up, grad_down)
```

```python
import jax
import jax.numpy as jnp
from jax import lax
from jax.sharding import PartitionSpec as P

BF = jnp.bfloat16
F32 = jnp.float32
GROUP_TOKENS = 48
FOUR = 4
CUTS_X = ((0, 1024), (1024, 2048))
CUTS_IN = ((0, 1024), (1024, 2048))
CUTS_OUT = ((0, 1024), (1024, 2048))


def dot(a, b, ca, cb, out=F32):
    return lax.dot_general(
        a, b, (((ca,), (cb,)), ((), ())), preferred_element_type=F32
    ).astype(out)


def routing(ids, gates, experts, groups, cap):
    count = ids.shape[0]
    per = experts // groups
    named = ids[:, :, None] == jnp.arange(experts, dtype=jnp.int32)[None, None, :]
    hit = jnp.any(named, axis=1)
    weight = jnp.sum(jnp.where(named, gates.astype(F32)[:, :, None], 0.0), axis=1)
    member = (
        lax.broadcasted_iota(jnp.int32, (experts, groups), 0) // per
        == lax.broadcasted_iota(jnp.int32, (experts, groups), 1)
    ).astype(BF)
    reach = dot(hit.astype(BF), member, 1, 0) > 0.5
    earlier = (
        lax.broadcasted_iota(jnp.int32, (count, count), 0)
        > lax.broadcasted_iota(jnp.int32, (count, count), 1)
    ).astype(BF)
    rank = dot(earlier, hit.astype(BF), 1, 0)
    code = jnp.where(hit & (rank < cap), rank, -1.0)
    place = jnp.where(reach, dot(earlier, reach.astype(BF), 1, 0), -1.0)
    return code.astype(BF), weight.astype(BF), place.T


def places(place):
    groups, count = place.shape
    at = lax.broadcasted_iota(jnp.int32, (groups, GROUP_TOKENS, count), 1).astype(F32)
    return (place[:, None, :] == at).astype(BF).reshape(groups * GROUP_TOKENS, count)


def columns_of(pick, table):
    return dot(pick, table, 1, 1)


def narrow_order(wide, narrow, cap, turn):
    size = wide * FOUR * cap
    new = lax.broadcasted_iota(jnp.int32, (size, size), 0)
    old = lax.broadcasted_iota(jnp.int32, (size, size), 1)
    n1, w, c = new // (wide * cap), new // cap % wide, new % cap
    return (old == ((w ^ turn) * FOUR + n1) * cap + c).astype(BF)


def reorder(perm, a):
    out = lax.dot_general(
        jnp.broadcast_to(perm, (a.shape[0],) + perm.shape),
        a,
        (((2,), (1,)), ((0,), (0,))),
        preferred_element_type=F32,
    )
    return out.astype(BF).reshape(-1, a.shape[2])


def local(tokens, out_grad, expert_ids, gates, w_gate, w_up, w_down, gate_saved, up_saved):
    wide = lax.axis_size("wide")
    narrow = lax.axis_size("narrow")
    devices = wide * narrow
    experts = devices // 2
    per = experts // wide
    count, width = tokens.shape
    hidden = gate_saved.shape[2]
    cap = gate_saved.shape[1] // devices
    rows = devices * cap
    held = wide * GROUP_TOKENS
    runs = narrow // FOUR
    me = lax.axis_index("wide")

    def swap(a, axis, parts):
        out = lax.all_to_all(
            a.reshape(parts, -1, a.shape[1]), axis, split_axis=0, concat_axis=0, tiled=True
        )
        return out.reshape(a.shape)

    code, weight, place = routing(expert_ids, gates, experts, wide, cap)
    sel = places(place)
    turned = (
        lax.broadcasted_iota(jnp.int32, (wide, wide), 0) ^ me
        == lax.broadcasted_iota(jnp.int32, (wide, wide), 1)
    ).astype(BF)
    sel_turned = places(dot(turned, place.astype(BF), 1, 0))

    sent = dot(sel, jnp.concatenate([out_grad, code, weight], axis=1), 1, 0, BF)
    got = swap(sent, "wide", wide)
    pick = (
        lax.broadcasted_iota(jnp.int32, (per, experts), 1)
        == lax.broadcasted_iota(jnp.int32, (per, experts), 0) + me * per
    ).astype(BF)
    got_code = columns_of(pick, got[:, width : width + experts])
    got_weight = columns_of(pick, got[:, width + experts :])
    row = lax.broadcasted_iota(jnp.int32, (2 * wide * cap, held), 0)
    col = lax.broadcasted_iota(jnp.int32, (2 * wide * cap, held), 1)
    own = row // cap % wide == col // GROUP_TOKENS
    slot = jnp.where(own, row % cap, -2).astype(F32)
    placed = got_code[:, None, :] == slot[None]
    spread = jnp.where(placed, got_weight[:, None, :], 0.0).astype(BF).reshape(rows, held)
    placed = placed.astype(BF).reshape(rows, held)
    rows_dy = []
    for low, high in CUTS_IN:
        rows_dy.append(swap(dot(spread, got[:, low:high], 1, 0, BF), "narrow", narrow))

    sent_x = dot(sel_turned, tokens, 1, 0, BF).reshape(wide, GROUP_TOKENS, width)
    got_x = jnp.zeros((wide, GROUP_TOKENS, width), BF)
    for k in range(wide):
        part = sent_x[k]
        if k:
            part = lax.ppermute(part, "wide", [(i, i ^ k) for i in range(wide)])
        got_x = lax.dynamic_update_slice_in_dim(got_x, part[None], me ^ k, 0)
    got_x = got_x.reshape(held, width)
    rows_x = [swap(dot(placed, got_x[:, a:b], 1, 0, BF), "narrow", narrow) for a, b in CUTS_X]

    def saved(a):
        a = a.reshape(wide, runs, FOUR * cap, hidden).transpose(1, 0, 2, 3)
        return reorder(narrow_order(wide, narrow, cap, 0), a.reshape(runs, -1, hidden)).astype(F32)

    gate_pre = saved(gate_saved[0])
    up_pre = saved(up_saved[0])
    sigma = jax.nn.sigmoid(gate_pre)
    silu = gate_pre * sigma
    act = (silu * up_pre).astype(BF)
    act_grad = sum(dot(dy, w_down[0, :, a:b], 1, 1) for dy, (a, b) in zip(rows_dy, CUTS_IN))
    up_grad = (act_grad * silu).astype(BF)
    gate_grad = (act_grad * up_pre * sigma * (1.0 + gate_pre * (1.0 - sigma))).astype(BF)
    token_grad = []
    for i, (a, b) in enumerate(CUTS_OUT):
        partial_value = dot(gate_grad, w_gate[0, a:b], 1, 1) + dot(up_grad, w_up[0, a:b], 1, 1)
        partial_value = partial_value.astype(BF)
        if i == 0:
            partial_value, *rows_x = lax.optimization_barrier((partial_value, *rows_x))
        arrived = swap(partial_value, "narrow", narrow)
        back = dot(placed, arrived, 0, 0, BF)
        if i + 1 < len(CUTS_OUT):
            back = back.reshape(wide, GROUP_TOKENS, b - a)
            parts = [lax.dynamic_index_in_dim(back, me, 0, False)]
            for k in range(1, wide):
                part = lax.dynamic_index_in_dim(back, me ^ k, 0, False)
                parts.append(lax.ppermute(part, "wide", [(i, i ^ k) for i in range(wide)]))
            token_grad.append(dot(sel_turned, jnp.concatenate(parts, axis=0), 0, 0, BF))
        else:
            token_grad.append(dot(sel, swap(back, "wide", wide), 0, 0, BF))
    token_grad = jnp.concatenate(token_grad, axis=1)

    grad_gate = jnp.concatenate([dot(x, gate_grad, 0, 0, BF) for x in rows_x], axis=0)
    grad_up = jnp.concatenate([dot(x, up_grad, 0, 0, BF) for x in rows_x], axis=0)
    grad_down = jnp.concatenate([dot(act, dy, 0, 0, BF) for dy in rows_dy], axis=1)
    return (token_grad, grad_gate[None], grad_up[None], grad_down[None])


def solution(mesh):
    both = ("wide", "narrow")
    flat, deep = P(both, None), P(both, None, None)
    return jax.shard_map(
        local,
        mesh=mesh,
        in_specs=(flat, flat, flat, flat, deep, deep, deep, deep, deep),
        out_specs=(flat, deep, deep, deep),
        check_vma=False,
    )
```

```python
import jax
import jax.numpy as jnp
from jax import lax
from jax.sharding import PartitionSpec as P

BF = jnp.bfloat16
F32 = jnp.float32
GROUP_TOKENS = 48
FOUR = 4
CUTS_X = ((0, 1024), (1024, 2048))
CUTS_IN = ((0, 1024), (1024, 2048))
CUTS_OUT = ((0, 1024), (1024, 2048))


def dot(a, b, ca, cb, out=F32):
    return lax.dot_general(
        a, b, (((ca,), (cb,)), ((), ())), preferred_element_type=F32
    ).astype(out)


def routing(ids, gates, experts, groups, cap):
    count = ids.shape[0]
    per = experts // groups
    named = ids[:, :, None] == jnp.arange(experts, dtype=jnp.int32)[None, None, :]
    hit = jnp.any(named, axis=1)
    weight = jnp.sum(jnp.where(named, gates.astype(F32)[:, :, None], 0.0), axis=1)
    member = (
        lax.broadcasted_iota(jnp.int32, (experts, groups), 0) // per
        == lax.broadcasted_iota(jnp.int32, (experts, groups), 1)
    ).astype(BF)
    reach = dot(hit.astype(BF), member, 1, 0) > 0.5
    earlier = (
        lax.broadcasted_iota(jnp.int32, (count, count), 0)
        > lax.broadcasted_iota(jnp.int32, (count, count), 1)
    ).astype(BF)
    rank = dot(earlier, hit.astype(BF), 1, 0)
    code = jnp.where(hit & (rank < cap), rank, -1.0)
    place = jnp.where(reach, dot(earlier, reach.astype(BF), 1, 0), -1.0)
    return code.astype(BF), weight.astype(BF), place.T


def places(place):
    groups, count = place.shape
    at = lax.broadcasted_iota(jnp.int32, (groups, GROUP_TOKENS, count), 1).astype(F32)
    return (place[:, None, :] == at).astype(BF).reshape(groups * GROUP_TOKENS, count)


def columns_of(pick, table):
    return dot(pick, table, 1, 1)


def narrow_order(wide, narrow, cap, turn):
    size = wide * FOUR * cap
    new = lax.broadcasted_iota(jnp.int32, (size, size), 0)
    old = lax.broadcasted_iota(jnp.int32, (size, size), 1)
    n1, w, c = new // (wide * cap), new // cap % wide, new % cap
    return (old == ((w ^ turn) * FOUR + n1) * cap + c).astype(BF)


def reorder(perm, a):
    out = lax.dot_general(
        jnp.broadcast_to(perm, (a.shape[0],) + perm.shape),
        a,
        (((2,), (1,)), ((0,), (0,))),
        preferred_element_type=F32,
    )
    return out.astype(BF).reshape(-1, a.shape[2])


def local(tokens, out_grad, expert_ids, gates, w_gate, w_up, w_down, gate_saved, up_saved):
    wide = lax.axis_size("wide")
    narrow = lax.axis_size("narrow")
    devices = wide * narrow
    experts = devices // 2
    per = experts // wide
    count, width = tokens.shape
    hidden = gate_saved.shape[2]
    cap = gate_saved.shape[1] // devices
    rows = devices * cap
    held = wide * GROUP_TOKENS
    runs = narrow // FOUR
    me = lax.axis_index("wide")

    def swap(a, axis, parts):
        out = lax.all_to_all(
            a.reshape(parts, -1, a.shape[1]), axis, split_axis=0, concat_axis=0, tiled=True
        )
        return out.reshape(a.shape)

    code, weight, place = routing(expert_ids, gates, experts, wide, cap)
    sel = places(place)
    turned = (
        lax.broadcasted_iota(jnp.int32, (wide, wide), 0) ^ me
        == lax.broadcasted_iota(jnp.int32, (wide, wide), 1)
    ).astype(BF)
    sel_turned = places(dot(turned, place.astype(BF), 1, 0))

    def to_groups(rows):
        rows = rows.reshape(wide, GROUP_TOKENS, -1)
        out = jnp.zeros_like(rows)
        for k in range(wide):
            part = rows[k]
            if k:
                part = lax.ppermute(part, "wide", [(i, i ^ k) for i in range(wide)])
            out = lax.dynamic_update_slice_in_dim(out, part[None], me ^ k, 0)
        return out.reshape(held, -1)

    sent = dot(sel, jnp.concatenate([code, weight, out_grad], axis=1), 1, 0, BF)
    got = swap(sent, "wide", wide)
    info = 2 * experts
    pick = (
        lax.broadcasted_iota(jnp.int32, (per, experts), 1)
        == lax.broadcasted_iota(jnp.int32, (per, experts), 0) + me * per
    ).astype(BF)
    got_code = columns_of(pick, got[:, :experts])
    got_weight = columns_of(pick, got[:, experts:info])
    row = lax.broadcasted_iota(jnp.int32, (2 * wide * cap, held), 0)
    col = lax.broadcasted_iota(jnp.int32, (2 * wide * cap, held), 1)
    own = row // cap % wide == col // GROUP_TOKENS
    slot = jnp.where(own, row % cap, -2).astype(F32)
    placed = got_code[:, None, :] == slot[None]
    spread = jnp.where(placed, got_weight[:, None, :], 0.0).astype(BF).reshape(rows, held)
    placed = placed.astype(BF).reshape(rows, held)
    slots = [dot(spread, got[:, info + a : info + b], 1, 0, BF) for a, b in CUTS_IN]
    rows_dy = [swap(part, "narrow", narrow) for part in slots]

    turned_x, slots[0] = lax.optimization_barrier((tokens, slots[0]))
    got_x = to_groups(dot(sel_turned, turned_x, 1, 0, BF))
    first, last = [dot(placed, got_x[:, a:b], 1, 0, BF) for a, b in CUTS_X]
    first, rows_dy[1] = lax.optimization_barrier((first, rows_dy[1]))
    rows_x = [swap(first, "narrow", narrow)]

    def saved(a):
        a = a.reshape(wide, runs, FOUR * cap, hidden).transpose(1, 0, 2, 3)
        return reorder(narrow_order(wide, narrow, cap, 0), a.reshape(runs, -1, hidden)).astype(F32)

    gate_pre = saved(gate_saved[0])
    up_pre = saved(up_saved[0])
    gate_pre, up_pre, rows_dy[1] = lax.optimization_barrier((gate_pre, up_pre, rows_dy[1]))
    sigma = jax.nn.sigmoid(gate_pre)
    silu = gate_pre * sigma
    act = (silu * up_pre).astype(BF)
    act_grad = sum(dot(dy, w_down[0, :, a:b], 1, 1) for dy, (a, b) in zip(rows_dy, CUTS_IN))
    up_grad = (act_grad * silu).astype(BF)
    gate_grad = (act_grad * up_pre * sigma * (1.0 + gate_pre * (1.0 - sigma))).astype(BF)
    back = []
    for a, b in CUTS_OUT:
        partial_value = dot(gate_grad, w_gate[0, a:b], 1, 1) + dot(up_grad, w_up[0, a:b], 1, 1)
        partial_value = partial_value.astype(BF)
        if a == 0:
            partial_value, rows_x[0] = lax.optimization_barrier((partial_value, rows_x[0]))
        else:
            partial_value, back[0] = lax.optimization_barrier((partial_value, back[0]))
        back.append(swap(partial_value, "narrow", narrow))
    last, back[1] = lax.optimization_barrier((last, back[1]))
    rows_x.append(swap(last, "narrow", narrow))

    back = jnp.concatenate([dot(placed, part, 0, 0, BF) for part in back], axis=1)
    back = back.reshape(wide, GROUP_TOKENS, width)
    parts = [lax.dynamic_index_in_dim(back, me, 0, False)]
    for k in range(1, wide):
        part = lax.dynamic_index_in_dim(back, me ^ k, 0, False)
        parts.append(lax.ppermute(part, "wide", [(i, i ^ k) for i in range(wide)]))
    token_grad = dot(sel_turned, jnp.concatenate(parts, axis=0), 0, 0, BF)
    rows_x[1], token_grad = lax.optimization_barrier((rows_x[1], token_grad))

    def by_rows(right):
        parts = [dot(x, right, 0, 0, BF) for x in rows_x]
        out = lax.optimization_barrier(jnp.concatenate([parts[0]] * len(parts), axis=0))
        return lax.dynamic_update_slice_in_dim(out, parts[1], CUTS_X[1][0], 0)

    grad_gate, grad_up = by_rows(gate_grad), by_rows(up_grad)
    grad_down = jnp.concatenate([dot(act, dy, 0, 0, BF) for dy in rows_dy], axis=1)
    return (token_grad, grad_gate[None], grad_up[None], grad_down[None])


def solution(mesh):
    both = ("wide", "narrow")
    flat, deep = P(both, None), P(both, None, None)
    return jax.shard_map(
        local,
        mesh=mesh,
        in_specs=(flat, flat, flat, flat, deep, deep, deep, deep, deep),
        out_specs=(flat, deep, deep, deep),
        check_vma=False,
    )
```

```python
import jax
import jax.numpy as jnp
import numpy as np
from jax import lax
from jax.sharding import PartitionSpec as P

BF = jnp.bfloat16
F32 = jnp.float32
GROUP = 16


def dot(a, b, ca, cb, out=F32):
    return lax.dot_general(
        a, b, (((ca,), (cb,)), ((), ())), preferred_element_type=F32
    ).astype(out)


def routing(ids, gates, experts, cap):
    count = ids.shape[0]
    named = ids.T[None, :, :] == jnp.arange(experts, dtype=jnp.int32)[:, None, None]
    hit = jnp.any(named, axis=1)
    weight = jnp.sum(jnp.where(named, gates.astype(F32).T[None, :, :], 0.0), axis=1)
    later = (
        lax.broadcasted_iota(jnp.int32, (count, count), 0)
        < lax.broadcasted_iota(jnp.int32, (count, count), 1)
    ).astype(BF)
    rank = dot(hit.astype(BF), later, 1, 0)
    return jnp.where(hit & (rank < cap), rank, -1.0), weight


def slot_tables(code, weight, cap):
    experts, count = code.shape
    wide_code = jnp.tile(jnp.repeat(code, 2, axis=0), (1, 2))[:, None, :]
    wide_weight = jnp.tile(jnp.repeat(weight, 2, axis=0), (1, 2))[:, None, :]
    row = lax.broadcasted_iota(jnp.int32, (2 * cap, 2 * count), 0)
    col = lax.broadcasted_iota(jnp.int32, (2 * cap, 2 * count), 1)
    slot = jnp.where(row // cap == col // count, row % cap, -2).astype(F32)
    hit = wide_code == slot[None]
    shape = (2 * experts * 2 * cap, 2 * count)
    placed = jnp.where(hit, 1.0, 0.0).astype(BF).reshape(shape)
    spread = jnp.where(hit, wide_weight, 0.0).astype(BF).reshape(shape)
    return placed, spread


def half_rows(cap, half):
    row = np.arange(GROUP * cap)
    want = (row // cap * 2 + half) * cap + row % cap
    return (np.arange(GROUP * 2 * cap)[None, :] == want[:, None]).astype(jnp.bfloat16)


def local(tokens, out_grad, expert_ids, gates, w_gate, w_up, w_down, gate_saved, up_saved):
    devices = lax.axis_size("wide") * lax.axis_size("narrow")
    experts = devices // 2
    count, width = tokens.shape
    cap = gate_saved.shape[1] // devices
    rows = devices * cap
    part = width // 2
    sides = [slice(0, part), slice(part, width)]
    picks = [jnp.asarray(half_rows(cap, half)) for half in range(2)]

    def stacked(a):
        return jnp.concatenate([a[:, side] for side in sides], axis=0)

    def swap(a):
        out = lax.all_to_all(
            a.reshape(devices, 2 * cap, part), ("wide", "narrow"), split_axis=0, concat_axis=0, tiled=True
        )
        return out.reshape(2 * rows, part)

    def grouped(pick, a, dim):
        a = a.reshape(devices // GROUP, -1, part)
        pick = jnp.broadcast_to(pick, (a.shape[0],) + pick.shape)
        out = lax.dot_general(
            pick, a, (((dim + 1,), (1,)), ((0,), (0,))), preferred_element_type=F32
        )
        return out.reshape(-1, part)

    def unpack(a):
        return [grouped(pick, a, 1).astype(BF) for pick in picks]

    code, weight = routing(expert_ids, gates, experts, cap)
    placed, spread = slot_tables(code, weight, cap)

    got_dy = swap(dot(spread, stacked(out_grad), 1, 0, BF))
    x_slots = dot(placed, stacked(tokens), 1, 0, BF)
    x_slots, got_dy = lax.optimization_barrier((x_slots, got_dy))
    got_x = swap(x_slots)

    rows_dy = unpack(got_dy)
    gate_pre = gate_saved[0].astype(F32)
    up_pre = up_saved[0].astype(F32)
    sigma = jax.nn.sigmoid(gate_pre)
    silu = gate_pre * sigma
    act = (silu * up_pre).astype(BF)
    act_grad = sum(dot(dy, w_down[0, :, side], 1, 1) for dy, side in zip(rows_dy, sides))
    up_grad = (act_grad * silu).astype(BF)
    gate_grad = (act_grad * up_pre * sigma * (1.0 + gate_pre * (1.0 - sigma))).astype(BF)
    slot_grad = [
        (dot(gate_grad, w_gate[0, side], 1, 1) + dot(up_grad, w_up[0, side], 1, 1)).astype(BF)
        for side in sides
    ]
    packed = sum(grouped(pick, a, 0) for pick, a in zip(picks, slot_grad)).astype(BF)
    packed, got_x = lax.optimization_barrier((packed, got_x))
    back = swap(packed)
    token_grad = dot(placed, back, 0, 0, BF)
    token_grad = jnp.concatenate([token_grad[:count], token_grad[count:]], axis=1)

    rows_x = unpack(got_x)
    grad_gate = jnp.concatenate([dot(x, gate_grad, 0, 0, BF) for x in rows_x], axis=0)
    grad_up = jnp.concatenate([dot(x, up_grad, 0, 0, BF) for x in rows_x], axis=0)
    grad_down = jnp.concatenate([dot(act, dy, 0, 0, BF) for dy in rows_dy], axis=1)
    return (token_grad, grad_gate[None], grad_up[None], grad_down[None])


def solution(mesh):
    both = ("wide", "narrow")
    flat, deep = P(both, None), P(both, None, None)
    return jax.shard_map(
        local,
        mesh=mesh,
        in_specs=(flat, flat, flat, flat, deep, deep, deep, deep, deep),
        out_specs=(flat, deep, deep, deep),
        check_vma=False,
    )
```

```python
import jax
import jax.numpy as jnp
import numpy as np
from jax import lax
from jax.experimental import pallas as pl
from jax.experimental.pallas import tpu as pltpu
from jax.sharding import PartitionSpec as P

BF = jnp.bfloat16
F32 = jnp.float32
GROUP = 16
BLOCK = 8


def dot(a, b, ca, cb, out=F32):
    return lax.dot_general(
        a, b, (((ca,), (cb,)), ((), ())), preferred_element_type=F32
    ).astype(out)


def slot_ranks(ids, experts, cap):
    choices, count = ids.shape
    expert = lax.broadcasted_iota(jnp.int32, (experts, count), 0)
    named = jnp.zeros((experts, count), F32)
    for k in range(choices):
        named = jnp.where(ids[k : k + 1] == expert, 1.0, named)
    later = (
        lax.broadcasted_iota(jnp.int32, (count, count), 0)
        < lax.broadcasted_iota(jnp.int32, (count, count), 1)
    )
    rank = dot(named.astype(BF), jnp.where(later, 1.0, 0.0).astype(BF), 1, 0)
    return jnp.where((named > 0.5) & (rank < cap), rank, -1.0)


def pick_rows(code, weight, cap):
    count = code.shape[1]
    row = lax.broadcasted_iota(jnp.int32, (2 * cap, 2 * count), 0)
    col = lax.broadcasted_iota(jnp.int32, (2 * cap, 2 * count), 1)
    slot = jnp.where(row < cap, jnp.where(col < count, row, -2), jnp.where(col < count, -2, row - cap))
    slot = slot.astype(F32)
    code = jnp.concatenate([code, code], axis=1)
    if weight is not None:
        weight = jnp.concatenate([weight, weight], axis=1)
    parts = []
    for e in range(code.shape[0]):
        worth = 1.0 if weight is None else weight[e : e + 1]
        parts += [jnp.where(code[e : e + 1] == slot, worth, 0.0)] * 2
    return jnp.concatenate(parts, axis=0).astype(BF)


def slot_kernel(experts, cap, scaled, ids, gates, values, out, stacked, rows, sems):
    count, width = values.shape
    part = width // 2
    choice = ids[...]
    code = slot_ranks(choice, experts, cap)
    weight = None
    if scaled:
        worth = gates[...].astype(F32)
        expert = lax.broadcasted_iota(jnp.int32, (experts, count), 0)
        weight = jnp.zeros((experts, count), F32)
        for k in range(choice.shape[0]):
            weight = jnp.where(choice[k : k + 1] == expert, worth[k : k + 1], weight)
    stacked[:count] = values[:, :part]
    stacked[count:] = values[:, part:]
    block = rows.shape[1]
    copies = []
    for i in range(experts // BLOCK):
        some = slice(i * BLOCK, (i + 1) * BLOCK)
        pick = pick_rows(code[some], weight[some] if scaled else None, cap)
        rows[i] = dot(pick, stacked[...], 1, 0, BF)
        copy = pltpu.make_async_copy(rows.at[i], out.at[pl.ds(i * block, block)], sems.at[i])
        copy.start()
        copies.append(copy)
    for copy in copies:
        copy.wait()


def slot_rows(ids, gates, values, experts, cap, scaled):
    count, width = values.shape
    part = width // 2
    blocks, block = experts // BLOCK, 4 * BLOCK * cap
    vmem = pl.BlockSpec(memory_space=pltpu.VMEM)
    return pl.pallas_call(
        lambda *refs: slot_kernel(experts, cap, scaled, *refs),
        in_specs=[vmem, vmem, vmem],
        out_specs=pl.BlockSpec(memory_space=pl.ANY),
        out_shape=jax.ShapeDtypeStruct((blocks * block, part), BF),
        scratch_shapes=[
            pltpu.VMEM((2 * count, part), BF),
            pltpu.VMEM((blocks, block, part), BF),
            pltpu.SemaphoreType.DMA((blocks,)),
        ],
        compiler_params=pltpu.CompilerParams(vmem_limit_bytes=56 * 2**20),
        cost_estimate=pl.CostEstimate(
            flops=2 * blocks * block * count * width,
            bytes_accessed=2 * blocks * block * part + 2 * count * width,
            transcendentals=0,
        ),
    )(ids, gates, values)


def sum_kernel(experts, cap, ids, back, out, rows, sems):
    count, width = out.shape
    part = width // 2
    blocks, block = rows.shape[:2]
    copies = [
        pltpu.make_async_copy(back.at[pl.ds(i * block, block)], rows.at[i], sems.at[i])
        for i in range(blocks)
    ]
    for copy in copies:
        copy.start()
    code = slot_ranks(ids[...], experts, cap)
    total = jnp.zeros((2 * count, part), F32)
    for i, copy in enumerate(copies):
        pick = pick_rows(code[i * BLOCK : (i + 1) * BLOCK], None, cap)
        copy.wait()
        total = total + dot(pick, rows[i], 0, 0)
    out[:, :part] = total[:count].astype(BF)
    out[:, part:] = total[count:].astype(BF)


def token_sums(ids, back, experts, cap):
    count = ids.shape[1]
    part = back.shape[1]
    blocks, block = experts // BLOCK, 4 * BLOCK * cap
    vmem = pl.BlockSpec(memory_space=pltpu.VMEM)
    return pl.pallas_call(
        lambda *refs: sum_kernel(experts, cap, *refs),
        in_specs=[vmem, pl.BlockSpec(memory_space=pl.ANY)],
        out_specs=vmem,
        out_shape=jax.ShapeDtypeStruct((count, 2 * part), BF),
        scratch_shapes=[
            pltpu.VMEM((blocks, block, part), BF),
            pltpu.SemaphoreType.DMA((blocks,)),
        ],
        compiler_params=pltpu.CompilerParams(vmem_limit_bytes=56 * 2**20),
        cost_estimate=pl.CostEstimate(
            flops=4 * blocks * block * count * part,
            bytes_accessed=2 * blocks * block * part,
            transcendentals=0,
        ),
    )(ids, back)


def half_rows(cap, half):
    row = np.arange(GROUP * cap)
    want = (row // cap * 2 + half) * cap + row % cap
    return (np.arange(GROUP * 2 * cap)[None, :] == want[:, None]).astype(jnp.bfloat16)


def local(tokens, out_grad, expert_ids, gates, w_gate, w_up, w_down, gate_saved, up_saved):
    devices = lax.axis_size("wide") * lax.axis_size("narrow")
    experts = devices // 2
    width = tokens.shape[1]
    cap = gate_saved.shape[1] // devices
    rows = devices * cap
    part = width // 2
    sides = [slice(0, part), slice(part, width)]
    picks = [jnp.asarray(half_rows(cap, half)) for half in range(2)]

    def swap(a):
        out = lax.all_to_all(
            a.reshape(devices, 2 * cap, part), ("wide", "narrow"), split_axis=0, concat_axis=0, tiled=True
        )
        return out.reshape(2 * rows, part)

    def grouped(pick, a, dim):
        a = a.reshape(devices // GROUP, -1, part)
        pick = jnp.broadcast_to(pick, (a.shape[0],) + pick.shape)
        out = lax.dot_general(
            pick, a, (((dim + 1,), (1,)), ((0,), (0,))), preferred_element_type=F32
        )
        return out.reshape(-1, part)

    def unpack(a):
        return [grouped(pick, a, 1).astype(BF) for pick in picks]

    ids, scales = expert_ids.T, gates.T
    got_dy = swap(slot_rows(ids, scales, out_grad, experts, cap, True))
    x_slots = slot_rows(ids, scales, tokens, experts, cap, False)
    x_slots, got_dy = lax.optimization_barrier((x_slots, got_dy))
    got_x = swap(x_slots)

    rows_dy = unpack(got_dy)
    gate_pre = gate_saved[0].astype(F32)
    up_pre = up_saved[0].astype(F32)
    sigma = jax.nn.sigmoid(gate_pre)
    silu = gate_pre * sigma
    act = (silu * up_pre).astype(BF)
    act_grad = sum(dot(dy, w_down[0, :, side], 1, 1) for dy, side in zip(rows_dy, sides))
    up_grad = (act_grad * silu).astype(BF)
    gate_grad = (act_grad * up_pre * sigma * (1.0 + gate_pre * (1.0 - sigma))).astype(BF)
    slot_grad = [
        (dot(gate_grad, w_gate[0, side], 1, 1) + dot(up_grad, w_up[0, side], 1, 1)).astype(BF)
        for side in sides
    ]
    packed = sum(grouped(pick, a, 0) for pick, a in zip(picks, slot_grad)).astype(BF)
    packed, got_x = lax.optimization_barrier((packed, got_x))
    back = swap(packed)
    token_grad = token_sums(ids, back, experts, cap)

    rows_x = unpack(got_x)
    grad_gate = jnp.concatenate([dot(x, gate_grad, 0, 0, BF) for x in rows_x], axis=0)
    grad_up = jnp.concatenate([dot(x, up_grad, 0, 0, BF) for x in rows_x], axis=0)
    grad_down = jnp.concatenate([dot(act, dy, 0, 0, BF) for dy in rows_dy], axis=1)
    return (token_grad, grad_gate[None], grad_up[None], grad_down[None])


def solution(mesh):
    both = ("wide", "narrow")
    flat, deep = P(both, None), P(both, None, None)
    return jax.shard_map(
        local,
        mesh=mesh,
        in_specs=(flat, flat, flat, flat, deep, deep, deep, deep, deep),
        out_specs=(flat, deep, deep, deep),
        check_vma=False,
    )
```

```python
import jax
import jax.numpy as jnp
import numpy as np
from jax import lax
from jax.experimental import pallas as pl
from jax.experimental.pallas import tpu as pltpu
from jax.sharding import PartitionSpec as P

BF = jnp.bfloat16
F32 = jnp.float32
GROUP = 16
BLOCK = 8


def dot(a, b, ca, cb, out=F32):
    return lax.dot_general(
        a, b, (((ca,), (cb,)), ((), ())), preferred_element_type=F32
    ).astype(out)


def slot_ranks(ids, experts, cap):
    choices, count = ids.shape
    expert = lax.broadcasted_iota(jnp.int32, (experts, count), 0)
    named = jnp.zeros((experts, count), F32)
    for k in range(choices):
        named = jnp.where(ids[k : k + 1] == expert, 1.0, named)
    later = (
        lax.broadcasted_iota(jnp.int32, (count, count), 0)
        < lax.broadcasted_iota(jnp.int32, (count, count), 1)
    )
    rank = dot(named.astype(BF), jnp.where(later, 1.0, 0.0).astype(BF), 1, 0)
    return jnp.where((named > 0.5) & (rank < cap), rank, -1.0)


def pick_rows(code, weight, cap):
    count = code.shape[1]
    row = lax.broadcasted_iota(jnp.int32, (2 * cap, 2 * count), 0)
    col = lax.broadcasted_iota(jnp.int32, (2 * cap, 2 * count), 1)
    slot = jnp.where(row < cap, jnp.where(col < count, row, -2), jnp.where(col < count, -2, row - cap))
    slot = slot.astype(F32)
    code = jnp.concatenate([code, code], axis=1)
    if weight is not None:
        weight = jnp.concatenate([weight, weight], axis=1)
    parts = []
    for e in range(code.shape[0]):
        worth = 1.0 if weight is None else weight[e : e + 1]
        parts += [jnp.where(code[e : e + 1] == slot, worth, 0.0)] * 2
    return jnp.concatenate(parts, axis=0).astype(BF)


def slot_kernel(experts, cap, scaled, ids, gates, values, out, stacked, rows, sems, load_sems):
    count, width = values.shape
    part = width // 2
    loads = [
        pltpu.make_async_copy(
            values.at[:, pl.ds(half * part, part)], stacked.at[pl.ds(half * count, count)], load_sems.at[half]
        )
        for half in range(2)
    ]
    for load in loads:
        load.start()
    choice = ids[...]
    code = slot_ranks(choice, experts, cap)
    weight = None
    if scaled:
        worth = gates[...].astype(F32)
        expert = lax.broadcasted_iota(jnp.int32, (experts, count), 0)
        weight = jnp.zeros((experts, count), F32)
        for k in range(choice.shape[0]):
            weight = jnp.where(choice[k : k + 1] == expert, worth[k : k + 1], weight)
    for load in loads:
        load.wait()
    block = rows.shape[1]
    copies = []
    for i in range(experts // BLOCK):
        some = slice(i * BLOCK, (i + 1) * BLOCK)
        pick = pick_rows(code[some], weight[some] if scaled else None, cap)
        rows[i] = dot(pick, stacked[...], 1, 0, BF)
        copy = pltpu.make_async_copy(rows.at[i], out.at[pl.ds(i * block, block)], sems.at[i])
        copy.start()
        copies.append(copy)
    for copy in copies:
        copy.wait()


def slot_rows(ids, gates, values, experts, cap, scaled):
    count, width = values.shape
    part = width // 2
    blocks, block = experts // BLOCK, 4 * BLOCK * cap
    vmem = pl.BlockSpec(memory_space=pltpu.VMEM)
    return pl.pallas_call(
        lambda *refs: slot_kernel(experts, cap, scaled, *refs),
        in_specs=[vmem, vmem, pl.BlockSpec(memory_space=pl.ANY)],
        out_specs=pl.BlockSpec(memory_space=pl.ANY),
        out_shape=jax.ShapeDtypeStruct((blocks * block, part), BF),
        scratch_shapes=[
            pltpu.VMEM((2 * count, part), BF),
            pltpu.VMEM((blocks, block, part), BF),
            pltpu.SemaphoreType.DMA((blocks,)),
            pltpu.SemaphoreType.DMA((2,)),
        ],
        compiler_params=pltpu.CompilerParams(vmem_limit_bytes=56 * 2**20),
        cost_estimate=pl.CostEstimate(
            flops=2 * blocks * block * count * width,
            bytes_accessed=2 * blocks * block * part + 2 * count * width,
            transcendentals=0,
        ),
    )(ids, gates, values)


def sum_kernel(experts, cap, ids, back, out, rows, sems):
    count, width = out.shape
    part = width // 2
    blocks = experts // BLOCK
    block = rows.shape[0] // blocks
    copies = []
    for i in range(blocks):
        place = pl.ds(i * block, block)
        copies.append(pltpu.make_async_copy(back.at[place], rows.at[place], sems.at[i]))
    for copy in copies:
        copy.start()
    code = slot_ranks(ids[...], experts, cap)
    total = jnp.zeros((2 * count, part), F32)
    for i in range(0, blocks, 2):
        pick = pick_rows(code[i * BLOCK : (i + 2) * BLOCK], None, cap)
        copies[i].wait()
        copies[i + 1].wait()
        total = total + dot(pick, rows[i * block : (i + 2) * block], 0, 0)
    out[:, :part] = total[:count].astype(BF)
    out[:, part:] = total[count:].astype(BF)


def token_sums(ids, back, experts, cap):
    count = ids.shape[1]
    part = back.shape[1]
    blocks, block = experts // BLOCK, 4 * BLOCK * cap
    vmem = pl.BlockSpec(memory_space=pltpu.VMEM)
    return pl.pallas_call(
        lambda *refs: sum_kernel(experts, cap, *refs),
        in_specs=[vmem, pl.BlockSpec(memory_space=pl.ANY)],
        out_specs=vmem,
        out_shape=jax.ShapeDtypeStruct((count, 2 * part), BF),
        scratch_shapes=[
            pltpu.VMEM((blocks * block, part), BF),
            pltpu.SemaphoreType.DMA((blocks,)),
        ],
        compiler_params=pltpu.CompilerParams(vmem_limit_bytes=56 * 2**20),
        cost_estimate=pl.CostEstimate(
            flops=4 * blocks * block * count * part,
            bytes_accessed=2 * blocks * block * part,
            transcendentals=0,
        ),
    )(ids, back)


def half_rows(cap, half):
    row = np.arange(GROUP * cap)
    want = (row // cap * 2 + half) * cap + row % cap
    return (np.arange(GROUP * 2 * cap)[None, :] == want[:, None]).astype(jnp.bfloat16)


def local(tokens, out_grad, expert_ids, gates, w_gate, w_up, w_down, gate_saved, up_saved):
    devices = lax.axis_size("wide") * lax.axis_size("narrow")
    experts = devices // 2
    width = tokens.shape[1]
    cap = gate_saved.shape[1] // devices
    rows = devices * cap
    part = width // 2
    sides = [slice(0, part), slice(part, width)]
    picks = [jnp.asarray(half_rows(cap, half)) for half in range(2)]

    def swap(a):
        out = lax.all_to_all(
            a.reshape(devices, 2 * cap, part), ("wide", "narrow"), split_axis=0, concat_axis=0, tiled=True
        )
        return out.reshape(2 * rows, part)

    def grouped(pick, a, dim):
        a = a.reshape(devices // GROUP, -1, part)
        pick = jnp.broadcast_to(pick, (a.shape[0],) + pick.shape)
        out = lax.dot_general(
            pick, a, (((dim + 1,), (1,)), ((0,), (0,))), preferred_element_type=F32
        )
        return out.reshape(-1, part)

    def unpack(a):
        return [grouped(pick, a, 1).astype(BF) for pick in picks]

    ids, scales = expert_ids.T, gates.T
    got_dy = swap(slot_rows(ids, scales, out_grad, experts, cap, True))
    x_slots = slot_rows(ids, scales, tokens, experts, cap, False)
    x_slots, got_dy = lax.optimization_barrier((x_slots, got_dy))
    got_x = swap(x_slots)

    rows_dy = unpack(got_dy)
    gate_pre = gate_saved[0].astype(F32)
    up_pre = up_saved[0].astype(F32)
    sigma = jax.nn.sigmoid(gate_pre)
    silu = gate_pre * sigma
    act = (silu * up_pre).astype(BF)
    act_grad = sum(dot(dy, w_down[0, :, side], 1, 1) for dy, side in zip(rows_dy, sides))
    up_grad = (act_grad * silu).astype(BF)
    gate_grad = (act_grad * up_pre * sigma * (1.0 + gate_pre * (1.0 - sigma))).astype(BF)
    slot_grad = [
        (dot(gate_grad, w_gate[0, side], 1, 1) + dot(up_grad, w_up[0, side], 1, 1)).astype(BF)
        for side in sides
    ]
    packed = sum(grouped(pick, a, 0) for pick, a in zip(picks, slot_grad)).astype(BF)
    packed, got_x = lax.optimization_barrier((packed, got_x))
    back = swap(packed)
    token_grad = token_sums(ids, back, experts, cap)

    rows_x = unpack(got_x)
    grad_gate = jnp.concatenate([dot(x, gate_grad, 0, 0, BF) for x in rows_x], axis=0)
    grad_up = jnp.concatenate([dot(x, up_grad, 0, 0, BF) for x in rows_x], axis=0)
    grad_down = jnp.concatenate([dot(act, dy, 0, 0, BF) for dy in rows_dy], axis=1)
    return (token_grad, grad_gate[None], grad_up[None], grad_down[None])


def solution(mesh):
    both = ("wide", "narrow")
    flat, deep = P(both, None), P(both, None, None)
    return jax.shard_map(
        local,
        mesh=mesh,
        in_specs=(flat, flat, flat, flat, deep, deep, deep, deep, deep),
        out_specs=(flat, deep, deep, deep),
        check_vma=False,
    )
```
